256 devices in a mesh: occ: 16 (over x_lo, z), aux: 16 (over y, x_hi, core).
Axes of the slice: x: 4 (x_hi: 2, x_lo: 2; x = x_hi * 2 + x_lo), y: 4, z: 8, core: 2. Of those that a mesh axis runs over, the one named last changes fastest.
Arguments:
- half_integrals: bfloat16 [16, 1024, 1024], P(None, 'aux'), may hold values from -1 to 1
- vir_coef: bfloat16 [1024, 768], P(None, 'occ'), may hold values from -0.1875 to 0.1875
- occ_energy: float32 [16], replicated, may hold values from -3 to -0.3
- vir_energy: float32 [768], replicated, may hold values from 0.1 to 2
Outputs:
- three_index: float32 [1024, 16, 768], P('aux', 'occ')
- vir_density: float32 [768, 768], P(('occ', 'aux'))
The draws below stay inside these ranges and needn't reach their ends.
All inputs are finite; a program needn't handle non-finite values.
Results may differ from the reference program's by a relative error of at most 0.0006.
The reference program's roundings to bfloat16 on the way (of `coupled` and `amplitude`) count: a program that leaves them out, or rounds other values in their place, can miss the bound.
Values may be sent and summed in bfloat16 or wider, within the bound.
No kernel may reach another device: no remote copies, remote signals or barrier semaphores. Data moves between devices by JAX's collectives and lax.ppermute only.
A program may use at most 64 MiB of HBM per device.

```python
import jax
import jax.numpy as jnp
from jax import lax

NBF = 1024
NV = 768
NAUX = 1024
NO = 16


def draw_occ_energy(key, part):
    offsets = jnp.arange(NO, dtype=jnp.int32).astype(jnp.float32)
    jitter = jax.random.uniform(key, (NO,), jnp.float32)
    return -3.0 + 2.7 * (offsets + jitter) / NO


def draw_vir_energy(key, part):
    offsets = jnp.arange(NV, dtype=jnp.int32).astype(jnp.float32)
    jitter = jax.random.uniform(jax.random.fold_in(key, 7), (NV,), jnp.float32)
    return 0.1 + 1.9 * (offsets + jitter) / NV


def block_scale(own_key, extent, pieces, smallest, top_value):
    def one(position, blocks):
        steps = jax.random.uniform(jax.random.fold_in(jax.random.fold_in(own_key, 6), position), (blocks,), jnp.float32, smallest / len(pieces), top_value / len(pieces))
        return jnp.repeat(jnp.exp(steps), extent[position] // blocks).reshape((-1,) + (1,) * (len(extent) - position - 1))

    gain = one(*pieces[0])
    for cut in pieces[1:]:
        gain = gain * one(*cut)
    return gain


def centred(stream_key, extent, deviation, limit, split=(), kind=jnp.bfloat16):
    level = block_scale(stream_key, extent, split, -0.22, 0.18) if split else 1.0
    result = jax.random.normal(stream_key, extent, jnp.float32) * deviation * level
    return jnp.minimum(jnp.maximum(result, -limit), limit).astype(kind)


def setup_inputs(seed: int = 0) -> dict:
    arg_keys = jax.random.split(jax.random.key(seed), 5)
    half_integrals = centred(arg_keys[0], (NO, NAUX, NBF), (NAUX ** -0.25), 1.0, ((1, 16),))
    vir_coef = centred(arg_keys[1], (NBF, NV), NBF ** -0.5, 0.1875, ((1, 16),))
    occ_energy = draw_occ_energy(jax.random.fold_in(arg_keys[4], 71), 0)
    vir_energy = draw_vir_energy(jax.random.fold_in(arg_keys[4], 71), 0)
    return dict(half_integrals=half_integrals, vir_coef=vir_coef, occ_energy=occ_energy, vir_energy=vir_energy)


def reference(half_integrals, vir_coef, occ_energy, vir_energy):
    coupled = jnp.einsum('ipm,ma->iap', half_integrals.astype(jnp.float32), vir_coef.astype(jnp.float32)).astype(jnp.bfloat16)
    coupled = lax.optimization_barrier(coupled)
    spread = coupled.astype(jnp.float32)

    def one_orbital(density, orbital):
        own_rows = lax.dynamic_index_in_dim(spread, orbital, 0, keepdims=False)
        coulomb = jnp.einsum('jbp,ap->jba', spread, own_rows)
        denominator = occ_energy[orbital] + occ_energy[:, None, None] - vir_energy[None, :, None] - vir_energy[None, None, :]
        amplitude = (coulomb / denominator).astype(jnp.bfloat16)
        amplitude = lax.optimization_barrier(amplitude).astype(jnp.float32)
        gamma_rows = jnp.einsum('jba,jbp->pa', amplitude, spread)
        density = density + jnp.einsum('jca,jcd->ad', amplitude, amplitude)
        return density, gamma_rows

    density, stacked = lax.scan(one_orbital, jnp.zeros((NV, NV), jnp.float32), jnp.arange(NO, dtype=jnp.int32))
    three_index = jnp.transpose(stacked, (1, 0, 2))
    return three_index, density / (NO * NV)
```

```python
import functools

import jax
import jax.numpy as jnp
import numpy as np
from jax import lax
from jax.experimental import pallas as pl
from jax.experimental.pallas import tpu as pltpu
from jax.sharding import Mesh, PartitionSpec as P

OCC = ("xl", "z")
CHIPS = ("y", "xh")
AUX = ("y", "xh", "c")
ALL = OCC + AUX
XL, Z, Y, XH, C = 2, 8, 4, 2, 2
NO, NV, NP = 16, 768, 1024
PW, VW = 64, 48
VMEM = pl.BlockSpec(memory_space=pltpu.VMEM)
SMEM = pl.BlockSpec(memory_space=pltpu.SMEM)


def swap(array, axis):
    return lax.ppermute(array, axis, [(0, 1), (1, 0)])


def ring(array, by):
    return lax.ppermute(array, "z", [(i, (i + by) % Z) for i in range(Z)])


def from_chip(array, dy, dx):
    pairs = [
        (y * XH + x, (y + dy) % Y * XH + (x + dx) % XH) for y in range(Y) for x in range(XH)
    ]
    return lax.ppermute(array, CHIPS, pairs)


def rows_of_slice(piece):
    xl, z = lax.axis_index("xl"), lax.axis_index("z")
    pair = jnp.concatenate([piece, swap(piece, "xl")], 0)
    blocks = [(pair, xl, z, 0)]
    up = down = pair
    for step in range(1, Z // 2):
        up, down = ring(up, 1), ring(down, -1)
        blocks += [(up, xl, z - step, 0), (down, xl, z + step, 0)]
    far = (z + Z // 2) % Z
    blocks += [(ring(up[:PW], 1), xl, far, 1), (ring(down[PW:], -1), 1 - xl, far, 1)]
    arrays, starts = [], []
    for array, lo, at, single in blocks:
        arrays.append(array)
        starts.append((lo * Z + at % Z) * PW)
        if not single:
            starts.append(((1 - lo) * Z + at % Z) * PW)
    return arrays, starts


def columns_of_block(local):
    y, xh, c = (lax.axis_index(n) for n in AUX)
    pieces, starts = [], []
    for dy in range(Y):
        for dx in range(XH):
            piece = from_chip(local, dy, dx) if dy or dx else local
            pieces.append(piece)
            starts.append((((y - dy) % Y) * XH + (xh - dx) % XH) * (C * PW))
    other = swap(jnp.stack(pieces), "c")
    return pieces + [other], [s + c * PW for s in starts] + [s + (1 - c) * PW for s in starts]


def work(n_rows, n_cols, starts_ref, *refs):
    row_refs, col_refs = refs[:n_rows], refs[n_rows : n_rows + n_cols]
    row_energy, col_energy, three_ref, vir_ref, rows, cols, amp = refs[n_rows + n_cols :]

    at = 0
    for ref in row_refs:
        for part in range(ref.shape[0] // PW):
            start = pl.multiple_of(starts_ref[at], PW)
            rows[pl.ds(start, PW), :] = ref[part * PW : (part + 1) * PW, :]
            at += 1
    for ref in col_refs:
        for part in range(ref.shape[0] if len(ref.shape) == 3 else 1):
            start = pl.multiple_of(starts_ref[at], PW)
            cols[pl.ds(start, PW), :] = ref[part] if len(ref.shape) == 3 else ref[...]
            at += 1

    transposed = (((0,), (0,)), ((), ()))
    block = 128

    @pl.loop(0, NV // block)
    def _(k):
        here = pl.ds(pl.multiple_of(k * block, block), block)
        coulomb = lax.dot_general(
            rows[:, here], cols[...], transposed, preferred_element_type=jnp.float32
        )
        amp[here, :] = (coulomb / (row_energy[here, :] - col_energy[...])).astype(jnp.bfloat16)

    step = 128

    @pl.loop(0, NP // step)
    def _(k):
        here = pl.ds(pl.multiple_of(k * step, step), step)
        three_ref[here, :] = jnp.dot(rows[here, :], amp[...], preferred_element_type=jnp.float32)

    @pl.loop(0, NV // block)
    def _(k):
        here = pl.ds(pl.multiple_of(k * block, block), block)
        vir_ref[here, :] = lax.dot_general(
            amp[:, here], amp[...], transposed, preferred_element_type=jnp.float32
        )


def per_device(half_integrals, vir_coef, occ_energy, vir_energy):
    xl, z, y, xh, c = (lax.axis_index(n) for n in ALL)
    own = xl * Z + z
    mine = (y * XH + xh) * C + c
    native = jnp.einsum(
        "ipm,ma->ipa", half_integrals, vir_coef, preferred_element_type=jnp.float32
    ).astype(jnp.bfloat16)

    flat = jnp.transpose(native, (1, 0, 2)).reshape(PW, NV)
    turned = lax.ppermute(flat, ALL, [(o * NO + x, x * NO + o) for o in range(NO) for x in range(NO)])
    row_arrays, row_starts = rows_of_slice(turned)

    local = lax.all_to_all(native, OCC, split_axis=0, concat_axis=0, tiled=True)
    local = jnp.transpose(local, (1, 0, 2)).reshape(PW, NV)
    col_arrays, col_starts = columns_of_block(local)

    slice_energy = lax.dynamic_slice_in_dim(vir_energy, mine * VW, VW, 0)
    own_energy = lax.dynamic_slice_in_dim(occ_energy, own, 1, 0)
    row_energy = ((own_energy + occ_energy)[:, None] - slice_energy[None, :]).reshape(NV, 1)
    starts = jnp.stack(row_starts + col_starts).astype(jnp.int32)

    three, vir = pl.pallas_call(
        functools.partial(work, len(row_arrays), len(col_arrays)),
        out_shape=[
            jax.ShapeDtypeStruct((NP, NV), jnp.float32),
            jax.ShapeDtypeStruct((NV, NV), jnp.float32),
        ],
        in_specs=[SMEM] + [VMEM] * (len(row_arrays) + len(col_arrays) + 2),
        out_specs=[VMEM, VMEM],
        scratch_shapes=[
            pltpu.VMEM((NP, NV), jnp.bfloat16),
            pltpu.VMEM((NP, NV), jnp.bfloat16),
            pltpu.VMEM((NV, NV), jnp.bfloat16),
        ],
        compiler_params=pltpu.CompilerParams(vmem_limit_bytes=40 * 2**20),
        cost_estimate=pl.CostEstimate(
            flops=4 * NV * NV * NP + 2 * NV**3, bytes_accessed=10 * 2**20, transcendentals=0
        ),
    )(starts, *row_arrays, *col_arrays, row_energy, vir_energy[None, :])

    three = three.reshape(Y * XH, C, PW, NV)
    keep = lax.dynamic_index_in_dim(three, c, 1, keepdims=False)
    give = lax.dynamic_index_in_dim(three, 1 - c, 1, keepdims=False)
    three = keep + swap(give, "c")
    three = lax.all_to_all(three, CHIPS, split_axis=0, concat_axis=0, tiled=True)
    three_index = jnp.sum(three, 0)[:, None, :]

    half = NV // C
    keep = lax.dynamic_slice_in_dim(vir, c * half, half, 1)
    give = lax.dynamic_slice_in_dim(vir, (1 - c) * half, half, 1)
    vir = (keep + swap(give, "c")).reshape(NO, VW, half)
    vir = lax.all_to_all(vir, OCC, split_axis=0, concat_axis=0, tiled=True)
    vir = jnp.sum(vir, 0).reshape(NO, VW // NO, half)
    vir = lax.all_to_all(vir, AUX, split_axis=0, concat_axis=0, tiled=True)
    vir = jnp.sum(vir.reshape(Y * XH, C, VW // NO, half), 0)
    vir_rows = jnp.concatenate([vir[0], vir[1]], 1)
    return (three_index, vir_rows / (NO * NV))


def solution(mesh):
    fine = Mesh(mesh.devices.reshape(XL, Z, Y, XH, C), ALL)
    return jax.shard_map(
        per_device,
        mesh=fine,
        in_specs=(P(None, AUX, None), P(None, OCC), P(), P()),
        out_specs=(P(AUX, OCC, None), P(ALL, None)),
        check_vma=False,
    )
```

```python
import functools

import jax
import jax.numpy as jnp
import numpy as np
from jax import lax
from jax.experimental import pallas as pl
from jax.experimental.pallas import tpu as pltpu
from jax.sharding import Mesh, PartitionSpec as P

OCC = ("xl", "z")
CHIPS = ("y", "xh")
AUX = ("y", "xh", "c")
ALL = OCC + AUX
XL, Z, Y, XH, C = 2, 8, 4, 2, 2
NO, NV, NP = 16, 768, 1024
PW, VW = 64, 48
VMEM = pl.BlockSpec(memory_space=pltpu.VMEM)
SMEM = pl.BlockSpec(memory_space=pltpu.SMEM)


def swap(array, axis):
    return lax.ppermute(array, axis, [(0, 1), (1, 0)])


def ring(array, by):
    return lax.ppermute(array, "z", [(i, (i + by) % Z) for i in range(Z)])


def next_chip(array, hop):
    pairs = [(q, hop_from(q, hop)) for q in range(Y * XH)]
    return lax.ppermute(array, CHIPS, pairs)


def hop_from(q, hop):
    return (q // XH + hop // XH) % Y * XH + (q + hop) % XH


def rows_of_slice(piece):
    xl, z = lax.axis_index("xl"), lax.axis_index("z")
    pair = jnp.concatenate([piece, swap(piece, "xl")], 0)
    arrays, owners = [pair], [(xl, z), (1 - xl, z)]
    up = down = pair
    first = None
    for step in range(1, Z // 2):
        up, down = ring(up, 1), ring(down, -1)
        first = up if first is None else first
        arrays += [up, down]
        owners += [(xl, z - step), (1 - xl, z - step), (xl, z + step), (1 - xl, z + step)]
    arrays += [ring(up[:PW], 1), ring(down[PW:], -1)]
    owners += [(xl, z + Z // 2), (1 - xl, z + Z // 2)]
    return arrays, [lo * Z + at % Z for lo, at in owners], first


TRANSPOSED = (((0,), (0,)), ((), ()))
HALF_P, HALF_V = NP // C, NV // C


def amplitudes(n_rows, place, *refs):
    row_refs, (own_cols, other_cols, row_energy, col_energy) = refs[:n_rows], refs[n_rows : n_rows + 4]
    rows, amp, vir, cols = refs[n_rows + 4 :]
    core = place[24]
    at = 0
    for ref in row_refs:
        for part in range(ref.shape[0] // PW):
            start = pl.multiple_of(place[at], PW)
            rows[pl.ds(start, PW), :] = ref[part * PW : (part + 1) * PW, :]
            at += 1
    cols[pl.ds(pl.multiple_of(core * HALF_P, HALF_P), HALF_P), :] = own_cols[...]
    cols[pl.ds(pl.multiple_of((1 - core) * HALF_P, HALF_P), HALF_P), :] = other_cols[...]
    for k in range(NV // 256):
        here = slice(k * 256, (k + 1) * 256)
        coulomb = lax.dot_general(
            rows[:, here], cols[...], TRANSPOSED, preferred_element_type=jnp.float32
        )
        amp[here, :] = (coulomb / (row_energy[here, :] - col_energy[...])).astype(jnp.bfloat16)
    virtual_block(amp, 1 - core, vir)


def virtual_block(amp, half, vir):
    side = amp[:, pl.ds(pl.multiple_of(half * HALF_V, HALF_V), HALF_V)]
    for k in range(NV // 256):
        here = slice(k * 256, (k + 1) * 256)
        vir[here, :] = lax.dot_general(
            amp[:, here], side, TRANSPOSED, preferred_element_type=jnp.float32
        )


def give_and_keep(place, rows, amp, vir, three):
    core = place[24]
    virtual_block(amp, core, vir)
    for k in range(HALF_P // 256):
        start = pl.multiple_of((1 - core) * HALF_P + k * 256, 256)
        three[k * 256 : (k + 1) * 256, :] = jnp.dot(
            rows[pl.ds(start, 256), :], amp[...], preferred_element_type=jnp.float32
        )


def pack_virtual(keep, got, out):
    total = keep[...] + got[...]
    top = jnp.maximum(jnp.max(jnp.abs(total), keepdims=True), 2.0**-100)
    power = jnp.ceil(jnp.log2(top))
    total = total * jnp.exp2(SCALE - power)
    tail = jnp.broadcast_to(power, (2, HALF_V))
    for g in range(NV // 6):
        out[8 * g : 8 * g + 8, :] = jnp.concatenate([total[6 * g : 6 * g + 6, :], tail], 0)


def keep_three(place, rows, amp, got, *outs):
    *outs, total = outs
    core = place[24]
    for k in range(HALF_P // 256):
        start = pl.multiple_of(core * HALF_P + k * 256, 256)
        here = slice(k * 256, (k + 1) * 256)
        total[here, :] = got[here, :] + jnp.dot(
            rows[pl.ds(start, 256), :], amp[...], preferred_element_type=jnp.float32
        )
    for hop, out in enumerate(outs):
        out[...] = total[pl.ds(pl.multiple_of(place[16 + hop], PW), PW), :]


SCALE = 14.0


def call(kernel, shapes, args, scratch=(), flops=0):
    return pl.pallas_call(
        kernel,
        out_shape=[jax.ShapeDtypeStruct(s, t) for s, t in shapes],
        in_specs=[SMEM if a.dtype == jnp.int32 else VMEM for a in args],
        out_specs=[VMEM] * len(shapes),
        scratch_shapes=[pltpu.VMEM(s, t) for s, t in scratch],
        compiler_params=pltpu.CompilerParams(vmem_limit_bytes=32 * 2**20),
        cost_estimate=pl.CostEstimate(flops=flops, bytes_accessed=6 * 2**20, transcendentals=0),
    )(*args)


def per_device(half_integrals, vir_coef, occ_energy, vir_energy):
    xl, z, y, xh, c = (lax.axis_index(n) for n in ALL)
    own = xl * Z + z
    chip = y * XH + xh
    native = jnp.einsum(
        "ipm,ma->ipa", half_integrals, vir_coef, preferred_element_type=jnp.float32
    ).astype(jnp.bfloat16)

    flat = jnp.transpose(native, (1, 0, 2)).reshape(PW, NV)
    turned = lax.ppermute(flat, ALL, [(o * NO + x, x * NO + o) for o in range(NO) for x in range(NO)])
    row_arrays, owners, first = rows_of_slice(turned)

    local = lax.all_to_all(native, OCC, split_axis=0, concat_axis=0, tiled=True)
    local = jnp.transpose(local, (1, 0, 2)).reshape(PW, NV)
    local, _ = lax.optimization_barrier((local, first))
    own_cols = lax.all_to_all(
        jnp.broadcast_to(local, (Y * XH, PW, NV)), CHIPS, split_axis=0, concat_axis=0, tiled=True
    ).reshape(HALF_P, NV)
    other_cols = swap(own_cols, "c")

    slice_energy = lax.dynamic_slice_in_dim(vir_energy, (chip * C + c) * VW, VW, 0)
    own_energy = lax.dynamic_slice_in_dim(occ_energy, own, 1, 0)
    row_energy = ((own_energy + occ_energy)[:, None] - slice_energy[None, :]).reshape(NV, 1)
    places = [o % C * HALF_P + o // C * PW for o in owners]
    places += [hop_from(chip, hop) * PW for hop in range(Y * XH)] + [c]
    place = jnp.stack(places).astype(jnp.int32)

    bf16, f32 = jnp.bfloat16, jnp.float32
    dot = 2 * NV * NV
    rows, amp, vir_give = call(
        functools.partial(amplitudes, len(row_arrays)),
        [((NP, NV), bf16), ((NV, NV), bf16), ((NV, HALF_V), f32)],
        [place, *row_arrays, own_cols, other_cols, row_energy, vir_energy[None, :]],
        [((NP, NV), bf16)],
        dot * (NP + HALF_V),
    )
    vir_got = swap(vir_give, "c")
    vir_keep, three_give = call(
        give_and_keep, [((NV, HALF_V), f32), ((HALF_P, NV), f32)], [place, rows, amp], (), dot * (HALF_V + HALF_P)
    )
    three_got = swap(three_give, "c")
    (packed,) = call(pack_virtual, [((NV // 6 * 8, HALF_V), f32)], [vir_keep, vir_got])
    sent = packed.astype(jnp.float16).reshape(NV // 6, 8, HALF_V)
    met = lax.all_to_all(sent, OCC + CHIPS, split_axis=0, concat_axis=0, tiled=True)

    pieces = call(
        keep_three,
        [((PW, NV), f32)] * (Y * XH),
        [place, rows, amp, three_got],
        [((HALF_P, NV), f32)],
        dot * HALF_P,
    )
    three = pieces[0]
    for hop in range(1, Y * XH):
        three = three + next_chip(pieces[hop], hop)
    three_index = three[:, None, :]

    met = met.astype(f32)
    weight = jnp.exp2(met[:, 6:7, :] - SCALE)
    vir = jnp.sum(met[:, :6, :] * weight, 0).reshape(C, 3, HALF_V)
    give, keep = jnp.where(c == 0, vir[1], vir[0]), jnp.where(c == 0, vir[0], vir[1])
    got = swap(give, "c")
    vir_rows = jnp.concatenate([jnp.where(c == 0, keep, got), jnp.where(c == 0, got, keep)], 1)
    return (three_index, vir_rows / (NO * NV))


def solution(mesh):
    fine = Mesh(mesh.devices.reshape(XL, Z, Y, XH, C), ALL)
    return jax.shard_map(
        per_device,
        mesh=fine,
        in_specs=(P(None, AUX, None), P(None, OCC), P(), P()),
        out_specs=(P(AUX, OCC, None), P(ALL, None)),
        check_vma=False,
    )
```

```python
import functools

import jax
import jax.numpy as jnp
import numpy as np
from jax import lax
from jax.experimental import pallas as pl
from jax.experimental.pallas import tpu as pltpu
from jax.sharding import Mesh, PartitionSpec as P

OCC = ("xl", "z")
CHIPS = ("y", "xh")
AUX = ("y", "xh", "c")
ALL = OCC + AUX
XL, Z, Y, XH, C = 2, 8, 4, 2, 2
NO, NV, NP = 16, 768, 1024
PW, VW = 64, 48
VMEM = pl.BlockSpec(memory_space=pltpu.VMEM)
SMEM = pl.BlockSpec(memory_space=pltpu.SMEM)


def swap(array, axis):
    return lax.ppermute(array, axis, [(0, 1), (1, 0)])


def ring(array, by):
    return lax.ppermute(array, "z", [(i, (i + by) % Z) for i in range(Z)])


def next_chip(array, hop):
    pairs = [(q, hop_from(q, hop)) for q in range(Y * XH)]
    return lax.ppermute(array, CHIPS, pairs)


def hop_from(q, hop):
    return (q // XH + hop // XH) % Y * XH + (q + hop) % XH


def paced(array, us):
    def kernel(given, out):
        out[...] = given[...]

    return pl.pallas_call(
        kernel,
        out_shape=jax.ShapeDtypeStruct(array.shape, array.dtype),
        in_specs=[VMEM],
        out_specs=VMEM,
        cost_estimate=pl.CostEstimate(flops=us * 10**9, bytes_accessed=2**20, transcendentals=0),
    )(array)


TRANSPOSED = (((0,), (0,)), ((), ()))
HALF_P, HALF_V = NP // C, NV // C


def amplitudes(n_rows, place, *refs):
    row_refs, (own_cols, other_cols, row_energy, col_energy) = refs[:n_rows], refs[n_rows : n_rows + 4]
    rows, amp, vir, cols, sems = refs[n_rows + 4 :]
    core = place[24]
    moves = []
    for ref in row_refs:
        for part in range(ref.shape[0] // PW):
            start = pl.multiple_of(place[len(moves)], PW)
            moves.append((ref.at[pl.ds(part * PW, PW)], rows.at[pl.ds(start, PW)]))
    for ref, side in ((own_cols, core), (other_cols, 1 - core)):
        moves.append((ref, cols.at[pl.ds(pl.multiple_of(side * HALF_P, HALF_P), HALF_P)]))
    copies = [pltpu.make_async_copy(f, t, sems.at[k]) for k, (f, t) in enumerate(moves)]
    for copy in copies:
        copy.start()
    for copy in copies:
        copy.wait()
    for k in range(NV // 256):
        here = slice(k * 256, (k + 1) * 256)
        coulomb = lax.dot_general(
            rows[:, here], cols[...], TRANSPOSED, preferred_element_type=jnp.float32
        )
        amp[here, :] = (coulomb / (row_energy[here, :] - col_energy[...])).astype(jnp.bfloat16)
    virtual_block(amp, 1 - core, vir)


def virtual_block(amp, half, vir):
    side = amp[:, pl.ds(pl.multiple_of(half * HALF_V, HALF_V), HALF_V)]
    for k in range(NV // 256):
        here = slice(k * 256, (k + 1) * 256)
        vir[here, :] = lax.dot_general(
            amp[:, here], side, TRANSPOSED, preferred_element_type=jnp.float32
        )


def give_and_keep(place, rows, amp, vir, give, keep):
    core = place[24]
    for out, side in ((give, 1 - core), (keep, core)):
        start = pl.multiple_of(side * HALF_P, HALF_P)
        out[...] = jnp.dot(rows[pl.ds(start, HALF_P), :], amp[...], preferred_element_type=jnp.float32)
    virtual_block(amp, core, vir)


def pack_virtual(keep, got, out):
    total = keep[...] + got[...]
    top = jnp.maximum(jnp.max(jnp.abs(total), keepdims=True), 2.0**-100)
    power = jnp.ceil(jnp.log2(top))
    total = total * jnp.exp2(SCALE - power)
    tail = jnp.broadcast_to(power, (8, HALF_V))
    for g in range(NO):
        out[g, :VW, :] = total[VW * g : VW * g + VW, :]
        out[g, VW:, :] = tail


def add_three(place, keep, got, *outs):
    *outs, total, sems = outs
    total[...] = keep[...] + got[...]
    copies = [
        pltpu.make_async_copy(total.at[pl.ds(pl.multiple_of(place[16 + hop], PW), PW)], out, sems.at[hop])
        for hop, out in enumerate(outs)
    ]
    for copy in copies:
        copy.start()
    for copy in copies:
        copy.wait()


SCALE = 14.0
PACE = 25


def call(kernel, shapes, args, scratch=(), flops=0, anywhere=0, n_sems=0, out_space=pltpu.VMEM):
    spaces = [SMEM if a.dtype == jnp.int32 else VMEM for a in args]
    first = 1 if args[0].dtype == jnp.int32 else 0
    spaces[first : first + anywhere] = [pl.BlockSpec(memory_space=pl.ANY)] * anywhere
    sems = [pltpu.SemaphoreType.DMA((n_sems,))] if n_sems else []
    return pl.pallas_call(
        kernel,
        out_shape=[jax.ShapeDtypeStruct(s, t) for s, t in shapes],
        in_specs=spaces,
        out_specs=[pl.BlockSpec(memory_space=out_space)] * len(shapes),
        scratch_shapes=[pltpu.VMEM(s, t) for s, t in scratch] + sems,
        compiler_params=pltpu.CompilerParams(vmem_limit_bytes=32 * 2**20),
        cost_estimate=pl.CostEstimate(flops=flops, bytes_accessed=6 * 2**20, transcendentals=0),
    )(*args)


def per_device(half_integrals, vir_coef, occ_energy, vir_energy):
    xl, z, y, xh, c = (lax.axis_index(n) for n in ALL)
    own = xl * Z + z
    chip = y * XH + xh
    native = jnp.einsum(
        "ipm,ma->ipa", half_integrals, vir_coef, preferred_element_type=jnp.float32
    ).astype(jnp.bfloat16)

    flat = jnp.transpose(native, (1, 0, 2)).reshape(PW, NV)
    pair = jnp.concatenate(
        [
            lax.ppermute(flat, ALL, [(o * NO + x, (x ^ flip) * NO + o) for o in range(NO) for x in range(NO)])
            for flip in (0, Z)
        ],
        0,
    )
    slice_energy = lax.dynamic_slice_in_dim(vir_energy, (chip * C + c) * VW, VW, 0)
    own_energy = lax.dynamic_slice_in_dim(occ_energy, own, 1, 0)
    row_energy = ((own_energy + occ_energy)[:, None] - slice_energy[None, :]).reshape(NV, 1)
    col_energy = vir_energy[None, :]

    pair, native, row_energy = lax.optimization_barrier((pair, native, row_energy))
    up1, down1, up2, down2 = (ring(pair, by) for by in (1, -1, 2, -2))
    row_energy = paced(row_energy, PACE)
    local = lax.all_to_all(native, OCC, split_axis=0, concat_axis=0, tiled=True)
    local = jnp.transpose(local, (1, 0, 2)).reshape(PW, NV)
    local, up2, down2, col_energy, row_energy = lax.optimization_barrier(
        (local, up2, down2, col_energy, row_energy)
    )
    up3, down3 = ring(up2, 1), ring(down2, -1)
    up4, down4 = ring(up2[:PW], 2), ring(down2[PW:], -2)
    col_energy = paced(col_energy, PACE)
    own_cols = lax.all_to_all(
        jnp.broadcast_to(local, (Y * XH, PW, NV)), CHIPS, split_axis=0, concat_axis=0, tiled=True
    ).reshape(HALF_P, NV)
    other_cols = swap(own_cols, "c")
    row_arrays = [pair, up1, down1, up2, down2, up3, down3, up4, down4]
    owners = []
    for step in (0, -1, 1, -2, 2, -3, 3, Z // 2):
        owners += [(xl * Z + (z + step) % Z), ((1 - xl) * Z + (z + step) % Z)]
    places = [o % C * HALF_P + o // C * PW for o in owners]
    places += [hop_from(chip, hop) * PW for hop in range(Y * XH)] + [c]
    place = jnp.stack(places).astype(jnp.int32)

    bf16, f32 = jnp.bfloat16, jnp.float32
    dot = 2 * NV * NV
    rows, amp, vir_give = call(
        functools.partial(amplitudes, len(row_arrays)),
        [((NP, NV), bf16), ((NV, NV), bf16), ((NV, HALF_V), f32)],
        [place, *row_arrays, own_cols, other_cols, row_energy, col_energy],
        [((NP, NV), bf16)],
        dot * (NP + HALF_V),
        len(row_arrays) + 2,
        NO + 2,
    )
    vir_got = swap(vir_give, "c")
    vir_keep, three_give, three_keep = call(
        give_and_keep,
        [((NV, HALF_V), f32), ((HALF_P, NV), f32), ((HALF_P, NV), f32)],
        [place, rows, amp],
        flops=dot * (HALF_V + NP),
    )
    three_got = swap(three_give, "c")
    (packed,) = call(pack_virtual, [((NO, VW + 8, HALF_V), f32)], [vir_keep, vir_got])
    met = lax.all_to_all(packed.astype(jnp.float16), OCC, split_axis=0, concat_axis=0, tiled=True)

    pieces = call(
        add_three,
        [((PW, NV), f32)] * (Y * XH),
        [place, three_keep, three_got],
        [((HALF_P, NV), f32)],
        n_sems=Y * XH,
        out_space=pltpu.HBM,
    )
    three = pieces[0]
    for hop in range(1, Y * XH):
        three = three + next_chip(pieces[hop], hop)
    three_index = three[:, None, :]

    met = met.astype(f32)
    vir = jnp.sum(met[:, :VW, :] * jnp.exp2(met[:, VW : VW + 1, :] - SCALE), 0)
    vir = vir.reshape(NO, VW // NO, HALF_V)
    vir = lax.all_to_all(vir, AUX, split_axis=0, concat_axis=0, tiled=True)
    vir = jnp.sum(vir.reshape(Y * XH, C, VW // NO, HALF_V), 0)
    vir_rows = jnp.concatenate([vir[0], vir[1]], 1)
    return (three_index, vir_rows / (NO * NV))


def solution(mesh):
    fine = Mesh(mesh.devices.reshape(XL, Z, Y, XH, C), ALL)
    return jax.shard_map(
        per_device,
        mesh=fine,
        in_specs=(P(None, AUX, None), P(None, OCC), P(), P()),
        out_specs=(P(AUX, OCC, None), P(ALL, None)),
        check_vma=False,
    )
```

```python
import functools

import jax
import jax.numpy as jnp
import numpy as np
from jax import lax
from jax.experimental import pallas as pl
from jax.experimental.pallas import tpu as pltpu
from jax.sharding import Mesh, PartitionSpec as P

OCC = ("xl", "z")
CHIPS = ("y", "xh")
AUX = ("y", "xh", "c")
ALL = OCC + AUX
XL, Z, Y, XH, C = 2, 8, 4, 2, 2
NO, NV, NP = 16, 768, 1024
PW, VW = 64, 48
VMEM = pl.BlockSpec(memory_space=pltpu.VMEM)
SMEM = pl.BlockSpec(memory_space=pltpu.SMEM)


def swap(array, axis):
    return lax.ppermute(array, axis, [(0, 1), (1, 0)])


def ring(array, by):
    return lax.ppermute(array, "z", [(i, (i + by) % Z) for i in range(Z)])


def next_chip(array, hop):
    pairs = [(q, hop_from(q, hop)) for q in range(Y * XH)]
    return lax.ppermute(array, CHIPS, pairs)


def hop_from(q, hop):
    return (q // XH + hop // XH) % Y * XH + (q + hop) % XH


def paced(array, us):
    def kernel(given, out):
        out[...] = given[...]

    return pl.pallas_call(
        kernel,
        out_shape=jax.ShapeDtypeStruct(array.shape, array.dtype),
        in_specs=[VMEM],
        out_specs=VMEM,
        compiler_params=pltpu.CompilerParams(vmem_limit_bytes=2**20),
        cost_estimate=pl.CostEstimate(flops=us * 10**9, bytes_accessed=2**20, transcendentals=0),
    )(array)


TRANSPOSED = (((0,), (0,)), ((), ()))
HALF_P, HALF_V = NP // C, NV // C


def amplitudes(n_rows, place, *refs):
    row_refs, (own_cols, other_cols, row_energy, col_energy) = refs[:n_rows], refs[n_rows : n_rows + 4]
    rows, amp, vir, cols, row_side, col_side, sems = refs[n_rows + 4 :]
    core = place[24]
    moves = []
    for ref in row_refs:
        for part in range(ref.shape[0] // PW):
            start = pl.multiple_of(place[len(moves)], PW)
            moves.append((ref.at[pl.ds(part * PW, PW)], rows.at[pl.ds(start, PW)]))
    for ref, side in ((own_cols, core), (other_cols, 1 - core)):
        moves.append((ref, cols.at[pl.ds(pl.multiple_of(side * HALF_P, HALF_P), HALF_P)]))
    moves += [(row_energy, row_side), (col_energy, col_side)]
    copies = [pltpu.make_async_copy(f, t, sems.at[k]) for k, (f, t) in enumerate(moves)]
    for copy in copies:
        copy.start()
    for copy in copies:
        copy.wait()
    for k in range(NV // 256):
        here = slice(k * 256, (k + 1) * 256)
        coulomb = lax.dot_general(
            rows[:, here], cols[...], TRANSPOSED, preferred_element_type=jnp.float32
        )
        amp[here, :] = (coulomb / (row_side[here, :] - col_side[...])).astype(jnp.bfloat16)
    virtual_block(amp, 1 - core, vir)


def virtual_block(amp, half, vir):
    side = amp[:, pl.ds(pl.multiple_of(half * HALF_V, HALF_V), HALF_V)]
    for k in range(NV // 256):
        here = slice(k * 256, (k + 1) * 256)
        vir[here, :] = lax.dot_general(
            amp[:, here], side, TRANSPOSED, preferred_element_type=jnp.float32
        )


def give_and_keep(place, rows, amp, give, keep):
    core = place[24]
    for out, side in ((give, 1 - core), (keep, core)):
        start = pl.multiple_of(side * HALF_P, HALF_P)
        out[...] = jnp.dot(rows[pl.ds(start, HALF_P), :], amp[...], preferred_element_type=jnp.float32)


def pack_virtual(place, amp, got, out, total):
    virtual_block(amp, place[24], total)
    total[...] += got[...]
    scale, power = scale_of(total[...])
    tail = jnp.broadcast_to(power, (8, HALF_V))
    for g in range(NO):
        out[g, :VW, :] = total[VW * g : VW * g + VW, :] * scale
        out[g, VW:, :] = tail


def add_three(place, keep, got, own, out, kept, met, sems):
    copies = [pltpu.make_async_copy(keep, kept, sems.at[0]), pltpu.make_async_copy(got, met, sems.at[1])]
    for copy in copies:
        copy.start()
    for copy in copies:
        copy.wait()
    kept[...] += met[...]
    scale, power = scale_of(kept[...])
    own[...] = kept[pl.ds(pl.multiple_of(place[16], PW), PW), :]
    for hop in range(1, Y * XH):
        out[hop - 1, :PW, :] = kept[pl.ds(pl.multiple_of(place[16 + hop], PW), PW), :] * scale
        out[hop - 1, PW:, :] = jnp.broadcast_to(power, (8, NV))


def scale_of(total):
    top = jnp.maximum(jnp.max(jnp.abs(total), keepdims=True), 2.0**-100)
    power = jnp.ceil(jnp.log2(top))
    return jnp.exp2(SCALE - power), power


def weight_of(sent, rows):
    power = lax.optimization_barrier(sent[..., rows : rows + 1, :])
    return jnp.exp2(power.astype(jnp.float32) - SCALE)


SCALE = 14.0
PACE = 25


def call(kernel, shapes, args, scratch=(), flops=0, anywhere=0, n_sems=0, space=pl.ANY):
    spaces = [SMEM if a.dtype == jnp.int32 else VMEM for a in args]
    first = 1 if args[0].dtype == jnp.int32 else 0
    spaces[first : first + anywhere] = [pl.BlockSpec(memory_space=space)] * anywhere
    sems = [pltpu.SemaphoreType.DMA((n_sems,))] if n_sems else []
    return pl.pallas_call(
        kernel,
        out_shape=[jax.ShapeDtypeStruct(s, t) for s, t in shapes],
        in_specs=spaces,
        out_specs=[VMEM] * len(shapes),
        scratch_shapes=[pltpu.VMEM(s, t) for s, t in scratch] + sems,
        compiler_params=pltpu.CompilerParams(vmem_limit_bytes=16 * 2**20),
        cost_estimate=pl.CostEstimate(flops=flops, bytes_accessed=6 * 2**20, transcendentals=0),
    )(*args)


def per_device(half_integrals, vir_coef, occ_energy, vir_energy):
    xl, z, y, xh, c = (lax.axis_index(n) for n in ALL)
    own = xl * Z + z
    chip = y * XH + xh
    native = jnp.einsum(
        "ipm,ma->ipa", half_integrals, vir_coef, preferred_element_type=jnp.float32
    ).astype(jnp.bfloat16)

    flat = jnp.transpose(native, (1, 0, 2)).reshape(PW, NV)
    pair = jnp.concatenate(
        [
            lax.ppermute(flat, ALL, [(o * NO + x, (x ^ flip) * NO + o) for o in range(NO) for x in range(NO)])
            for flip in (0, Z)
        ],
        0,
    )
    slice_energy = lax.dynamic_slice_in_dim(vir_energy, (chip * C + c) * VW, VW, 0)
    own_energy = lax.dynamic_slice_in_dim(occ_energy, own, 1, 0)
    row_energy = ((own_energy + occ_energy)[:, None] - slice_energy[None, :]).reshape(NV, 1)
    col_energy = vir_energy[None, :]

    local = lax.all_to_all(native, OCC, split_axis=0, concat_axis=0, tiled=True)
    row_energy = paced(row_energy, PACE)
    pair, local, row_energy = lax.optimization_barrier((pair, local, row_energy))
    local = jnp.transpose(local, (1, 0, 2)).reshape(PW, NV)
    up1, down1, up2, down2 = (ring(pair, by) for by in (1, -1, 2, -2))
    own_cols = lax.all_to_all(
        jnp.broadcast_to(local, (Y * XH, PW, NV)), CHIPS, split_axis=0, concat_axis=0, tiled=True
    ).reshape(HALF_P, NV)
    row_energy, col_energy, local = lax.optimization_barrier((row_energy, col_energy, local))
    col_energy = paced(col_energy, PACE)
    up2, down2, col_energy = lax.optimization_barrier((up2, down2, col_energy))
    col_energy = paced(col_energy, PACE)
    up3, down3 = ring(up2, 1), ring(down2, -1)
    up4, down4 = ring(up2[:PW], 2), ring(down2[PW:], -2)
    other_cols = swap(own_cols, "c")
    row_arrays = [pair, up1, down1, up2, down2, up3, down3, up4, down4]
    owners = []
    for step in (0, -1, 1, -2, 2, -3, 3, Z // 2):
        owners += [(xl * Z + (z + step) % Z), ((1 - xl) * Z + (z + step) % Z)]
    places = [o % C * HALF_P + o // C * PW for o in owners]
    places += [hop_from(chip, hop) * PW for hop in range(Y * XH)] + [c]
    place = jnp.stack(places).astype(jnp.int32)

    bf16, f32 = jnp.bfloat16, jnp.float32
    dot = 2 * NV * NV
    rows, amp, vir_give = call(
        functools.partial(amplitudes, len(row_arrays)),
        [((NP, NV), bf16), ((NV, NV), bf16), ((NV, HALF_V), f32)],
        [place, *row_arrays, own_cols, other_cols, row_energy, col_energy],
        [((NP, NV), bf16), ((NV, 1), f32), ((1, NV), f32)],
        dot * (NP + HALF_V),
        len(row_arrays) + 4,
        NO + 4,
        pltpu.HBM,
    )
    vir_got = swap(vir_give, "c")
    three_give, three_keep = call(
        give_and_keep,
        [((HALF_P, NV), f32)] * 2,
        [place, rows, amp],
        flops=dot * NP,
    )
    vir_got, three_give = lax.optimization_barrier((vir_got, three_give))
    three_got = swap(three_give, "c")
    (packed,) = call(
        pack_virtual,
        [((NO, VW + 8, HALF_V), f32)],
        [place, amp, vir_got],
        [((NV, HALF_V), f32)],
        dot * HALF_V,
    )
    packed, three_keep = lax.optimization_barrier((packed.astype(jnp.float16), three_keep))
    met = lax.all_to_all(packed, OCC, split_axis=0, concat_axis=0, tiled=True)
    own_piece, pieces = call(
        add_three,
        [((PW, NV), f32), ((Y * XH - 1, PW + 8, NV), f32)],
        [place, three_keep, three_got],
        [((HALF_P, NV), f32)] * 2,
        anywhere=2,
        n_sems=2,
    )
    got = [next_chip(piece.astype(jnp.float16), hop) for hop, piece in enumerate(pieces, 1)]
    met, *got = lax.optimization_barrier((met, *got))
    vir = jnp.sum(met[:, :VW].astype(f32) * weight_of(met, VW), 0)
    vir, *got = lax.optimization_barrier((vir, *got))
    weights = weight_of(jnp.concatenate([piece[PW:] for piece in got], 1), 0)
    three = own_piece
    for k, piece in enumerate(got):
        three = three + piece[:PW].astype(f32) * weights[:, k * NV : (k + 1) * NV]
    three_index = three[:, None, :]

    vir = vir.reshape(NO, VW // NO, HALF_V)
    vir = lax.all_to_all(vir, AUX, split_axis=0, concat_axis=0, tiled=True)
    vir = jnp.sum(vir.reshape(Y * XH, C, VW // NO, HALF_V), 0)
    vir_rows = jnp.concatenate([vir[0], vir[1]], 1)
    return (three_index, vir_rows / (NO * NV))


def solution(mesh):
    fine = Mesh(mesh.devices.reshape(XL, Z, Y, XH, C), ALL)
    return jax.shard_map(
        per_device,
        mesh=fine,
        in_specs=(P(None, AUX, None), P(None, OCC), P(), P()),
        out_specs=(P(AUX, OCC, None), P(ALL, None)),
        check_vma=False,
    )
```

```python
import functools

import jax
import jax.numpy as jnp
import numpy as np
from jax import lax
from jax.experimental import pallas as pl
from jax.experimental.pallas import tpu as pltpu
from jax.sharding import Mesh, PartitionSpec as P

OCC = ("xl", "z")
CHIPS = ("y", "xh")
AUX = ("y", "xh", "c")
ALL = OCC + AUX
XL, Z, Y, XH, C = 2, 8, 4, 2, 2
NO, NV, NP = 16, 768, 1024
PW, VW = 64, 48
VMEM = pl.BlockSpec(memory_space=pltpu.VMEM)
SMEM = pl.BlockSpec(memory_space=pltpu.SMEM)


def swap(array, axis):
    return lax.ppermute(array, axis, [(0, 1), (1, 0)])


def ring(array, by):
    return lax.ppermute(array, "z", [(i, (i + by) % Z) for i in range(Z)])


def next_chip(array, hop):
    pairs = [(q, hop_from(q, hop)) for q in range(Y * XH)]
    return lax.ppermute(array, CHIPS, pairs)


def hop_from(q, hop):
    return (q // XH + hop // XH) % Y * XH + (q + hop) % XH


def paced(array, us):
    def kernel(given, out):
        out[...] = given[...]

    return pl.pallas_call(
        kernel,
        out_shape=jax.ShapeDtypeStruct(array.shape, array.dtype),
        in_specs=[VMEM],
        out_specs=VMEM,
        compiler_params=pltpu.CompilerParams(vmem_limit_bytes=2**20),
        cost_estimate=pl.CostEstimate(flops=us * 10**9, bytes_accessed=2**20, transcendentals=0),
    )(array)


TRANSPOSED = (((0,), (0,)), ((), ()))
HALF_P, HALF_V = NP // C, NV // C


def amplitudes(n_rows, place, *refs):
    row_refs, (own_cols, other_cols, row_energy, col_energy) = refs[:n_rows], refs[n_rows : n_rows + 4]
    rows, amp, vir, cols, row_side, col_side, sems = refs[n_rows + 4 :]
    core = place[24]
    moves = []
    for ref in row_refs:
        for part in range(ref.shape[0] // PW):
            start = pl.multiple_of(place[len(moves)], PW)
            moves.append((ref.at[pl.ds(part * PW, PW)], rows.at[pl.ds(start, PW)]))
    for ref, side in ((own_cols, core), (other_cols, 1 - core)):
        moves.append((ref, cols.at[pl.ds(pl.multiple_of(side * HALF_P, HALF_P), HALF_P)]))
    moves += [(row_energy, row_side), (col_energy, col_side)]
    copies = [pltpu.make_async_copy(f, t, sems.at[k]) for k, (f, t) in enumerate(moves)]
    for copy in copies:
        copy.start()
    for copy in copies:
        copy.wait()
    for k in range(NV // 256):
        here = slice(k * 256, (k + 1) * 256)
        coulomb = lax.dot_general(
            rows[:, here], cols[...], TRANSPOSED, preferred_element_type=jnp.float32
        )
        amp[here, :] = (coulomb / (row_side[here, :] - col_side[...])).astype(jnp.bfloat16)
    virtual_block(amp, 1 - core, vir)


def virtual_block(amp, half, vir):
    side = amp[:, pl.ds(pl.multiple_of(half * HALF_V, HALF_V), HALF_V)]
    for k in range(NV // 256):
        here = slice(k * 256, (k + 1) * 256)
        vir[here, :] = lax.dot_general(
            amp[:, here], side, TRANSPOSED, preferred_element_type=jnp.float32
        )


def give_and_keep(place, rows, amp, give, keep):
    core = place[24]
    for out, side in ((give, 1 - core), (keep, core)):
        start = pl.multiple_of(side * HALF_P, HALF_P)
        out[...] = jnp.dot(rows[pl.ds(start, HALF_P), :], amp[...], preferred_element_type=jnp.float32)


def pack_virtual(place, amp, got, out, total):
    virtual_block(amp, place[24], total)
    total[...] += got[...]
    scale, power = scale_of(total[...])
    tail = jnp.broadcast_to(power, (8, HALF_V))
    for g in range(NO):
        out[g, :VW, :] = total[VW * g : VW * g + VW, :] * scale
        out[g, VW:, :] = tail


def add_three(place, keep, got, own, out, kept, met, sems):
    copies = [pltpu.make_async_copy(keep, kept, sems.at[0]), pltpu.make_async_copy(got, met, sems.at[1])]
    for copy in copies:
        copy.start()
    for copy in copies:
        copy.wait()
    kept[...] += met[...]
    scale, power = scale_of(kept[...])
    own[...] = kept[pl.ds(pl.multiple_of(place[16], PW), PW), :]
    for hop in range(1, Y * XH):
        out[hop - 1, :PW, :] = kept[pl.ds(pl.multiple_of(place[16 + hop], PW), PW), :] * scale
        out[hop - 1, PW:, :] = jnp.broadcast_to(power, (8, NV))


def sum_three(own, *refs):
    *got, out = refs
    total = own[...]
    for ref in got:
        total += ref[:PW, :] * jnp.exp2(ref[PW : PW + 1, :] - SCALE)
    out[...] = total


def scale_of(total):
    top = jnp.maximum(jnp.max(jnp.abs(total), keepdims=True), 2.0**-100)
    power = jnp.ceil(jnp.log2(top))
    return jnp.exp2(SCALE - power), power


def weight_of(sent, rows):
    power = lax.optimization_barrier(sent[..., rows : rows + 1, :])
    return jnp.exp2(power.astype(jnp.float32) - SCALE)


SCALE = 14.0
PACE = 25


def call(kernel, shapes, args, scratch=(), flops=0, anywhere=0, n_sems=0, space=pl.ANY):
    spaces = [SMEM if a.dtype == jnp.int32 else VMEM for a in args]
    first = 1 if args[0].dtype == jnp.int32 else 0
    spaces[first : first + anywhere] = [pl.BlockSpec(memory_space=space)] * anywhere
    sems = [pltpu.SemaphoreType.DMA((n_sems,))] if n_sems else []
    return pl.pallas_call(
        kernel,
        out_shape=[jax.ShapeDtypeStruct(s, t) for s, t in shapes],
        in_specs=spaces,
        out_specs=[VMEM] * len(shapes),
        scratch_shapes=[pltpu.VMEM(s, t) for s, t in scratch] + sems,
        compiler_params=pltpu.CompilerParams(vmem_limit_bytes=16 * 2**20),
        cost_estimate=pl.CostEstimate(flops=flops, bytes_accessed=6 * 2**20, transcendentals=0),
    )(*args)


def per_device(half_integrals, vir_coef, occ_energy, vir_energy):
    xl, z, y, xh, c = (lax.axis_index(n) for n in ALL)
    own = xl * Z + z
    chip = y * XH + xh
    native = jnp.einsum(
        "ipm,ma->ipa", half_integrals, vir_coef, preferred_element_type=jnp.float32
    ).astype(jnp.bfloat16)

    flat = jnp.transpose(native, (1, 0, 2)).reshape(PW, NV)
    pair = jnp.concatenate(
        [
            lax.ppermute(flat, ALL, [(o * NO + x, (x ^ flip) * NO + o) for o in range(NO) for x in range(NO)])
            for flip in (0, Z)
        ],
        0,
    )
    slice_energy = lax.dynamic_slice_in_dim(vir_energy, (chip * C + c) * VW, VW, 0)
    own_energy = lax.dynamic_slice_in_dim(occ_energy, own, 1, 0)
    row_energy = ((own_energy + occ_energy)[:, None] - slice_energy[None, :]).reshape(NV, 1)
    col_energy = vir_energy[None, :]

    local = lax.all_to_all(native, OCC, split_axis=0, concat_axis=0, tiled=True)
    row_energy = paced(row_energy, PACE)
    pair, local, row_energy = lax.optimization_barrier((pair, local, row_energy))
    local = jnp.transpose(local, (1, 0, 2)).reshape(PW, NV)
    up1, down1, up2, down2 = (ring(pair, by) for by in (1, -1, 2, -2))
    own_cols = lax.all_to_all(
        jnp.broadcast_to(local, (Y * XH, PW, NV)), CHIPS, split_axis=0, concat_axis=0, tiled=True
    ).reshape(HALF_P, NV)
    row_energy, col_energy, local = lax.optimization_barrier((row_energy, col_energy, local))
    col_energy = paced(col_energy, PACE)
    up2, down2, col_energy = lax.optimization_barrier((up2, down2, col_energy))
    col_energy = paced(col_energy, PACE)
    up3, down3 = ring(up2, 1), ring(down2, -1)
    up4, down4 = ring(up2[:PW], 2), ring(down2[PW:], -2)
    other_cols = swap(own_cols, "c")
    row_arrays = [pair, up1, down1, up2, down2, up3, down3, up4, down4]
    owners = []
    for step in (0, -1, 1, -2, 2, -3, 3, Z // 2):
        owners += [(xl * Z + (z + step) % Z), ((1 - xl) * Z + (z + step) % Z)]
    places = [o % C * HALF_P + o // C * PW for o in owners]
    places += [hop_from(chip, hop) * PW for hop in range(Y * XH)] + [c]
    place = jnp.stack(places).astype(jnp.int32)

    bf16, f32 = jnp.bfloat16, jnp.float32
    dot = 2 * NV * NV
    rows, amp, vir_give = call(
        functools.partial(amplitudes, len(row_arrays)),
        [((NP, NV), bf16), ((NV, NV), bf16), ((NV, HALF_V), f32)],
        [place, *row_arrays, own_cols, other_cols, row_energy, col_energy],
        [((NP, NV), bf16), ((NV, 1), f32), ((1, NV), f32)],
        dot * (NP + HALF_V),
        len(row_arrays) + 4,
        NO + 4,
        pltpu.HBM,
    )
    vir_got = swap(vir_give, "c")
    three_give, three_keep = call(
        give_and_keep,
        [((HALF_P, NV), f32)] * 2,
        [place, rows, amp],
        flops=dot * NP,
    )
    vir_got, three_give = lax.optimization_barrier((vir_got, three_give))
    three_got = swap(three_give, "c")
    (packed,) = call(
        pack_virtual,
        [((NO, VW + 8, HALF_V), f32)],
        [place, amp, vir_got],
        [((NV, HALF_V), f32)],
        dot * HALF_V,
    )
    packed, three_keep = lax.optimization_barrier((packed.astype(jnp.float16), three_keep))
    met = lax.all_to_all(packed, OCC, split_axis=0, concat_axis=0, tiled=True)
    own_piece, pieces = call(
        add_three,
        [((PW, NV), f32), ((Y * XH - 1, PW + 8, NV), f32)],
        [place, three_keep, three_got],
        [((HALF_P, NV), f32)] * 2,
        anywhere=2,
        n_sems=2,
    )
    got = [next_chip(piece.astype(jnp.float16), hop) for hop, piece in enumerate(pieces, 1)]
    met, *got[3:] = lax.optimization_barrier((met, *got[3:]))
    vir = jnp.sum(met[:, :VW].astype(f32) * weight_of(met, VW), 0)
    vir, *got[3:] = lax.optimization_barrier((vir, *got[3:]))
    got = [piece.astype(f32) for piece in got]
    (three,) = call(sum_three, [((PW, NV), f32)], [own_piece, *got])
    three_index = three[:, None, :]

    vir = vir.reshape(NO, VW // NO, HALF_V)
    vir = lax.all_to_all(vir, AUX, split_axis=0, concat_axis=0, tiled=True)
    vir = jnp.sum(vir.reshape(Y * XH, C, VW // NO, HALF_V), 0)
    vir_rows = jnp.concatenate([vir[0], vir[1]], 1)
    return (three_index, vir_rows / (NO * NV))


def solution(mesh):
    fine = Mesh(mesh.devices.reshape(XL, Z, Y, XH, C), ALL)
    return jax.shard_map(
        per_device,
        mesh=fine,
        in_specs=(P(None, AUX, None), P(None, OCC), P(), P()),
        out_specs=(P(AUX, OCC, None), P(ALL, None)),
        check_vma=False,
    )
```

```python
import functools

import jax
import jax.numpy as jnp
import numpy as np
from jax import lax
from jax.experimental import pallas as pl
from jax.experimental.pallas import tpu as pltpu
from jax.sharding import Mesh, PartitionSpec as P

OCC = ("xl", "z")
CHIPS = ("y", "xh")
AUX = ("y", "xh", "c")
ALL = OCC + AUX
XL, Z, Y, XH, C = 2, 8, 4, 2, 2
NO, NV, NP = 16, 768, 1024
PW, VW = 64, 48
VMEM = pl.BlockSpec(memory_space=pltpu.VMEM)
SMEM = pl.BlockSpec(memory_space=pltpu.SMEM)


def swap(array, axis):
    return lax.ppermute(array, axis, [(0, 1), (1, 0)])


def ring(array, by):
    pairs = [
        (z * C + c, (z + (1 - 2 * c) * by) % Z * C + c) for z in range(Z) for c in range(C)
    ]
    return lax.ppermute(array, ("z", "c"), pairs)


def next_chip(array, hop):
    pairs = [(q, hop_from(q, hop)) for q in range(Y * XH)]
    return lax.ppermute(array, CHIPS, pairs)


def hop_from(q, hop):
    return (q // XH + hop // XH) % Y * XH + (q + hop) % XH


def paced(array, us):
    def kernel(given, out):
        out[...] = given[...]

    return pl.pallas_call(
        kernel,
        out_shape=jax.ShapeDtypeStruct(array.shape, array.dtype),
        in_specs=[VMEM],
        out_specs=VMEM,
        compiler_params=pltpu.CompilerParams(vmem_limit_bytes=2**20),
        cost_estimate=pl.CostEstimate(flops=us * 10**9, bytes_accessed=2**20, transcendentals=0),
    )(array)


TRANSPOSED = (((0,), (0,)), ((), ()))
HALF_P, HALF_V = NP // C, NV // C


def amplitudes(n_rows, place, *refs):
    row_refs, (own_cols, other_cols, row_energy, col_energy) = refs[:n_rows], refs[n_rows : n_rows + 4]
    rows, amp, vir, cols, row_side, col_side, sems = refs[n_rows + 4 :]
    core = place[24]
    moves = []
    for ref in row_refs:
        for part in range(ref.shape[0] // PW):
            start = pl.multiple_of(place[len(moves)], PW)
            moves.append((ref.at[pl.ds(part * PW, PW)], rows.at[pl.ds(start, PW)]))
    for ref, side in ((own_cols, core), (other_cols, 1 - core)):
        moves.append((ref, cols.at[pl.ds(pl.multiple_of(side * HALF_P, HALF_P), HALF_P)]))
    moves += [(row_energy, row_side), (col_energy, col_side)]
    copies = [pltpu.make_async_copy(f, t, sems.at[k]) for k, (f, t) in enumerate(moves)]
    for copy in copies:
        copy.start()
    for copy in copies:
        copy.wait()
    for k in range(NV // 384):
        here = slice(k * 384, (k + 1) * 384)
        coulomb = lax.dot_general(
            rows[:, here], cols[...], TRANSPOSED, preferred_element_type=jnp.float32
        )
        amp[here, :] = (coulomb / (row_side[here, :] - col_side[...])).astype(jnp.bfloat16)
    virtual_block(amp, 1 - core, vir)


def virtual_block(amp, half, vir):
    side = amp[:, pl.ds(pl.multiple_of(half * HALF_V, HALF_V), HALF_V)]
    for k in range(NV // 384):
        here = slice(k * 384, (k + 1) * 384)
        vir[here, :] = lax.dot_general(
            amp[:, here], side, TRANSPOSED, preferred_element_type=jnp.float32
        )


def give_and_keep(place, rows, amp, give, keep):
    core = place[24]
    for out, side in ((give, 1 - core), (keep, core)):
        start = pl.multiple_of(side * HALF_P, HALF_P)
        out[...] = jnp.dot(rows[pl.ds(start, HALF_P), :], amp[...], preferred_element_type=jnp.float32)


def pack_virtual(place, amp, got, out, total):
    virtual_block(amp, place[24], total)
    total[...] += got[...]
    scale, power = scale_of(total[...])
    tail = jnp.broadcast_to(power, (8, HALF_V))
    for g in range(NO):
        out[g, :VW, :] = total[VW * g : VW * g + VW, :] * scale
        out[g, VW:, :] = tail


def add_three(place, keep, got, own, out, kept, met, sems):
    copies = [pltpu.make_async_copy(keep, kept, sems.at[0]), pltpu.make_async_copy(got, met, sems.at[1])]
    for copy in copies:
        copy.start()
    for copy in copies:
        copy.wait()
    kept[...] += met[...]
    scale, power = scale_of(kept[...])
    own[...] = kept[pl.ds(pl.multiple_of(place[16], PW), PW), :]
    for hop in range(1, Y * XH):
        out[hop - 1, :PW, :] = kept[pl.ds(pl.multiple_of(place[16 + hop], PW), PW), :] * scale
        out[hop - 1, PW:, :] = jnp.broadcast_to(power, (8, NV))


def sum_three(own, *refs):
    *got, out = refs
    total = own[...]
    for ref in got:
        total += ref[:PW, :] * jnp.exp2(ref[PW : PW + 1, :] - SCALE)
    out[...] = total


def scale_of(total):
    top = jnp.maximum(jnp.max(jnp.abs(total), keepdims=True), 2.0**-100)
    power = jnp.ceil(jnp.log2(top))
    return jnp.exp2(SCALE - power), power


def weight_of(sent, rows):
    power = lax.optimization_barrier(sent[..., rows : rows + 1, :])
    return jnp.exp2(power.astype(jnp.float32) - SCALE)


SCALE = 14.0
PACE = 25


def call(kernel, shapes, args, scratch=(), flops=0, anywhere=0, n_sems=0, space=pl.ANY):
    spaces = [SMEM if a.dtype == jnp.int32 else VMEM for a in args]
    first = 1 if args[0].dtype == jnp.int32 else 0
    spaces[first : first + anywhere] = [pl.BlockSpec(memory_space=space)] * anywhere
    sems = [pltpu.SemaphoreType.DMA((n_sems,))] if n_sems else []
    return pl.pallas_call(
        kernel,
        out_shape=[jax.ShapeDtypeStruct(s, t) for s, t in shapes],
        in_specs=spaces,
        out_specs=[VMEM] * len(shapes),
        scratch_shapes=[pltpu.VMEM(s, t) for s, t in scratch] + sems,
        compiler_params=pltpu.CompilerParams(vmem_limit_bytes=16 * 2**20),
        cost_estimate=pl.CostEstimate(flops=flops, bytes_accessed=6 * 2**20, transcendentals=0),
    )(*args)


def per_device(half_integrals, vir_coef, occ_energy, vir_energy):
    xl, z, y, xh, c = (lax.axis_index(n) for n in ALL)
    own = xl * Z + z
    chip = y * XH + xh
    native = jnp.einsum(
        "ipm,ma->ipa", half_integrals, vir_coef, preferred_element_type=jnp.float32
    ).astype(jnp.bfloat16)

    flat = jnp.transpose(native, (1, 0, 2)).reshape(PW, NV)
    pair = jnp.concatenate(
        [
            lax.ppermute(flat, ALL, [(o * NO + x, (x ^ flip) * NO + o) for o in range(NO) for x in range(NO)])
            for flip in (0, Z)
        ],
        0,
    )
    slice_energy = lax.dynamic_slice_in_dim(vir_energy, (chip * C + c) * VW, VW, 0)
    own_energy = lax.dynamic_slice_in_dim(occ_energy, own, 1, 0)
    row_energy = ((own_energy + occ_energy)[:, None] - slice_energy[None, :]).reshape(NV, 1)
    col_energy = vir_energy[None, :]

    local = lax.all_to_all(native, OCC, split_axis=0, concat_axis=0, tiled=True)
    row_energy = paced(row_energy, PACE)
    pair, local, row_energy = lax.optimization_barrier((pair, local, row_energy))
    local = jnp.transpose(local, (1, 0, 2)).reshape(PW, NV)
    up1, down1, up2, down2 = (ring(pair, by) for by in (1, -1, 2, -2))
    own_cols = lax.all_to_all(
        jnp.broadcast_to(local, (Y * XH, PW, NV)), CHIPS, split_axis=0, concat_axis=0, tiled=True
    ).reshape(HALF_P, NV)
    row_energy, col_energy, local = lax.optimization_barrier((row_energy, col_energy, local))
    col_energy = paced(col_energy, PACE)
    up2, down2, col_energy = lax.optimization_barrier((up2, down2, col_energy))
    col_energy = paced(col_energy, PACE)
    up3, down3, far = ring(up2, 1), ring(down2, -1), ring(up2, 2)
    other_cols = swap(own_cols, "c")
    row_arrays = [pair, up1, down1, up2, down2, up3, down3, far]
    owners = []
    for step in (0, -1, 1, -2, 2, -3, 3, Z // 2):
        at = (z + (1 - 2 * c) * step) % Z
        owners += [xl * Z + at, (1 - xl) * Z + at]
    places = [o % C * HALF_P + o // C * PW for o in owners]
    places += [hop_from(chip, hop) * PW for hop in range(Y * XH)] + [c]
    place = jnp.stack(places).astype(jnp.int32)

    bf16, f32 = jnp.bfloat16, jnp.float32
    dot = 2 * NV * NV
    rows, amp, vir_give = call(
        functools.partial(amplitudes, len(row_arrays)),
        [((NP, NV), bf16), ((NV, NV), bf16), ((NV, HALF_V), f32)],
        [place, *row_arrays, own_cols, other_cols, row_energy, col_energy],
        [((NP, NV), bf16), ((NV, 1), f32), ((1, NV), f32)],
        dot * (NP + HALF_V),
        len(row_arrays) + 4,
        NO + 4,
        pltpu.HBM,
    )
    vir_got = swap(vir_give, "c")
    three_give, three_keep = call(
        give_and_keep,
        [((HALF_P, NV), f32)] * 2,
        [place, rows, amp],
        flops=dot * NP,
    )
    vir_got, three_give = lax.optimization_barrier((vir_got, three_give))
    three_got = swap(three_give, "c")
    (packed,) = call(
        pack_virtual,
        [((NO, VW + 8, HALF_V), f32)],
        [place, amp, vir_got],
        [((NV, HALF_V), f32)],
        dot * HALF_V,
    )
    packed, three_keep = lax.optimization_barrier((packed.astype(jnp.float16), three_keep))
    met = lax.all_to_all(packed, OCC, split_axis=0, concat_axis=0, tiled=True)
    own_piece, pieces = call(
        add_three,
        [((PW, NV), f32), ((Y * XH - 1, PW + 8, NV), f32)],
        [place, three_keep, three_got],
        [((HALF_P, NV), f32)] * 2,
        anywhere=2,
        n_sems=2,
    )
    got = [next_chip(piece.astype(jnp.float16), hop) for hop, piece in enumerate(pieces, 1)]
    met, *got[3:] = lax.optimization_barrier((met, *got[3:]))
    vir = jnp.sum(met[:, :VW].astype(f32) * weight_of(met, VW), 0)
    vir, *got[3:] = lax.optimization_barrier((vir, *got[3:]))
    got = [piece.astype(f32) for piece in got]
    (three,) = call(sum_three, [((PW, NV), f32)], [own_piece, *got])
    three_index = three[:, None, :]

    vir = vir.reshape(NO, VW // NO, HALF_V)
    vir = lax.all_to_all(vir, AUX, split_axis=0, concat_axis=0, tiled=True)
    vir = jnp.sum(vir.reshape(Y * XH, C, VW // NO, HALF_V), 0)
    vir_rows = jnp.concatenate([vir[0], vir[1]], 1)
    return (three_index, vir_rows / (NO * NV))


def solution(mesh):
    fine = Mesh(mesh.devices.reshape(XL, Z, Y, XH, C), ALL)
    return jax.shard_map(
        per_device,
        mesh=fine,
        in_specs=(P(None, AUX, None), P(None, OCC), P(), P()),
        out_specs=(P(AUX, OCC, None), P(ALL, None)),
        check_vma=False,
    )
```

```python
import functools

import jax
import jax.numpy as jnp
import numpy as np
from jax import lax
from jax.experimental import pallas as pl
from jax.experimental.pallas import tpu as pltpu
from jax.sharding import Mesh, PartitionSpec as P

OCC = ("xl", "z")
CHIPS = ("y", "xh")
AUX = ("y", "xh", "c")
ALL = OCC + AUX
XL, Z, Y, XH, C = 2, 8, 4, 2, 2
NO, NV, NP = 16, 768, 1024
PW, VW = 64, 48
VMEM = pl.BlockSpec(memory_space=pltpu.VMEM)
SMEM = pl.BlockSpec(memory_space=pltpu.SMEM)


def swap(array, axis):
    return lax.ppermute(array, axis, [(0, 1), (1, 0)])


def ring(array, by):
    pairs = [
        (z * C + c, (z + (1 - 2 * c) * by) % Z * C + c) for z in range(Z) for c in range(C)
    ]
    return lax.ppermute(array, ("z", "c"), pairs)


def next_chip(array, hop):
    pairs = [(q * C + c, hop_from(q, hop, c) * C + c) for q in range(Y * XH) for c in range(C)]
    return lax.ppermute(array, AUX, pairs)


def hop_from(q, hop, c):
    return (q // XH + (1 - 2 * c) * (hop // XH)) % Y * XH + (q + hop) % XH


def paced(array, us):
    def kernel(given, out):
        out[...] = given[...]

    return pl.pallas_call(
        kernel,
        out_shape=jax.ShapeDtypeStruct(array.shape, array.dtype),
        in_specs=[VMEM],
        out_specs=VMEM,
        compiler_params=pltpu.CompilerParams(vmem_limit_bytes=2**20),
        cost_estimate=pl.CostEstimate(flops=us * 10**9, bytes_accessed=2**20, transcendentals=0),
    )(array)


TRANSPOSED = (((0,), (0,)), ((), ()))
HALF_P, HALF_V = NP // C, NV // C


def amplitudes(n_rows, place, *refs):
    row_refs, (own_cols, other_cols, row_energy, col_energy) = refs[:n_rows], refs[n_rows : n_rows + 4]
    rows, amp, vir, cols, row_side, col_side, sems = refs[n_rows + 4 :]
    core = place[24]
    moves = []
    for ref in row_refs:
        for part in range(ref.shape[0] // PW):
            start = pl.multiple_of(place[len(moves)], PW)
            moves.append((ref.at[pl.ds(part * PW, PW)], rows.at[pl.ds(start, PW)]))
    for ref, side in ((own_cols, core), (other_cols, 1 - core)):
        moves.append((ref, cols.at[pl.ds(pl.multiple_of(side * HALF_P, HALF_P), HALF_P)]))
    moves += [(row_energy, row_side), (col_energy, col_side)]
    copies = [pltpu.make_async_copy(f, t, sems.at[k]) for k, (f, t) in enumerate(moves)]
    for copy in copies:
        copy.start()
    for copy in copies:
        copy.wait()
    for k in range(NV // 384):
        here = slice(k * 384, (k + 1) * 384)
        coulomb = lax.dot_general(
            rows[:, here], cols[...], TRANSPOSED, preferred_element_type=jnp.float32
        )
        amp[here, :] = (coulomb / (row_side[here, :] - col_side[...])).astype(jnp.bfloat16)
    virtual_block(amp, 1 - core, vir)


def virtual_block(amp, half, vir):
    side = amp[:, pl.ds(pl.multiple_of(half * HALF_V, HALF_V), HALF_V)]
    for k in range(NV // 384):
        here = slice(k * 384, (k + 1) * 384)
        vir[here, :] = lax.dot_general(
            amp[:, here], side, TRANSPOSED, preferred_element_type=jnp.float32
        )


def give_and_keep(place, rows, amp, give, keep):
    core = place[24]
    for out, side in ((give, 1 - core), (keep, core)):
        start = pl.multiple_of(side * HALF_P, HALF_P)
        out[...] = jnp.dot(rows[pl.ds(start, HALF_P), :], amp[...], preferred_element_type=jnp.float32)


def pack_virtual(place, amp, got, out, total):
    virtual_block(amp, place[24], total)
    total[...] += got[...]
    scale, power = scale_of(total[...])
    tail = jnp.broadcast_to(power, (8, HALF_V))
    for g in range(NO):
        out[g, :VW, :] = total[VW * g : VW * g + VW, :] * scale
        out[g, VW:, :] = tail


def add_three(place, keep, got, own, out, kept, met, sems):
    copies = [pltpu.make_async_copy(keep, kept, sems.at[0]), pltpu.make_async_copy(got, met, sems.at[1])]
    for copy in copies:
        copy.start()
    for copy in copies:
        copy.wait()
    kept[...] += met[...]
    scale, power = scale_of(kept[...])
    own[...] = kept[pl.ds(pl.multiple_of(place[16], PW), PW), :]
    for hop in range(1, Y * XH):
        out[hop - 1, :PW, :] = kept[pl.ds(pl.multiple_of(place[16 + hop], PW), PW), :] * scale
        out[hop - 1, PW:, :] = jnp.broadcast_to(power, (8, NV))


def sum_three(own, *refs):
    *got, out = refs
    total = own[...]
    for ref in got:
        total += ref[:PW, :] * jnp.exp2(ref[PW : PW + 1, :] - SCALE)
    out[...] = total


def scale_of(total):
    top = jnp.maximum(jnp.max(jnp.abs(total), keepdims=True), 2.0**-100)
    power = jnp.ceil(jnp.log2(top))
    return jnp.exp2(SCALE - power), power


def weight_of(sent, rows):
    power = lax.optimization_barrier(sent[..., rows : rows + 1, :])
    return jnp.exp2(power.astype(jnp.float32) - SCALE)


SCALE = 14.0
PACE = 25


def call(kernel, shapes, args, scratch=(), flops=0, anywhere=0, n_sems=0, space=pl.ANY):
    spaces = [SMEM if a.dtype == jnp.int32 else VMEM for a in args]
    first = 1 if args[0].dtype == jnp.int32 else 0
    spaces[first : first + anywhere] = [pl.BlockSpec(memory_space=space)] * anywhere
    sems = [pltpu.SemaphoreType.DMA((n_sems,))] if n_sems else []
    return pl.pallas_call(
        kernel,
        out_shape=[jax.ShapeDtypeStruct(s, t) for s, t in shapes],
        in_specs=spaces,
        out_specs=[VMEM] * len(shapes),
        scratch_shapes=[pltpu.VMEM(s, t) for s, t in scratch] + sems,
        compiler_params=pltpu.CompilerParams(vmem_limit_bytes=16 * 2**20),
        cost_estimate=pl.CostEstimate(flops=flops, bytes_accessed=6 * 2**20, transcendentals=0),
    )(*args)


def per_device(half_integrals, vir_coef, occ_energy, vir_energy):
    xl, z, y, xh, c = (lax.axis_index(n) for n in ALL)
    own = xl * Z + z
    chip = y * XH + xh
    native = jnp.einsum(
        "ipm,ma->ipa", half_integrals, vir_coef, preferred_element_type=jnp.float32
    ).astype(jnp.bfloat16)

    flat = jnp.transpose(native, (1, 0, 2)).reshape(PW, NV)
    pair = jnp.concatenate(
        [
            lax.ppermute(flat, ALL, [(o * NO + x, (x ^ flip) * NO + o) for o in range(NO) for x in range(NO)])
            for flip in (0, Z)
        ],
        0,
    )
    slice_energy = lax.dynamic_slice_in_dim(vir_energy, (chip * C + c) * VW, VW, 0)
    own_energy = lax.dynamic_slice_in_dim(occ_energy, own, 1, 0)
    row_energy = ((own_energy + occ_energy)[:, None] - slice_energy[None, :]).reshape(NV, 1)
    col_energy = vir_energy[None, :]

    local = lax.all_to_all(native, OCC, split_axis=0, concat_axis=0, tiled=True)
    row_energy = paced(row_energy, PACE)
    pair, local, row_energy = lax.optimization_barrier((pair, local, row_energy))
    local = jnp.transpose(local, (1, 0, 2)).reshape(PW, NV)
    up1, down1, up2, down2 = (ring(pair, by) for by in (1, -1, 2, -2))
    own_cols = lax.all_to_all(
        jnp.broadcast_to(local, (Y * XH, PW, NV)), CHIPS, split_axis=0, concat_axis=0, tiled=True
    ).reshape(HALF_P, NV)
    row_energy, col_energy, local = lax.optimization_barrier((row_energy, col_energy, local))
    col_energy = paced(col_energy, PACE)
    up2, down2, col_energy = lax.optimization_barrier((up2, down2, col_energy))
    col_energy = paced(col_energy, PACE)
    up3, down3, far = ring(up2, 1), ring(down2, -1), ring(up2, 2)
    other_cols = swap(own_cols, "c")
    row_arrays = [pair, up1, down1, up2, down2, up3, down3, far]
    owners = []
    for step in (0, -1, 1, -2, 2, -3, 3, Z // 2):
        at = (z + (1 - 2 * c) * step) % Z
        owners += [xl * Z + at, (1 - xl) * Z + at]
    places = [o % C * HALF_P + o // C * PW for o in owners]
    places += [hop_from(chip, hop, c) * PW for hop in range(Y * XH)] + [c]
    place = jnp.stack(places).astype(jnp.int32)

    bf16, f32 = jnp.bfloat16, jnp.float32
    dot = 2 * NV * NV
    rows, amp, vir_give = call(
        functools.partial(amplitudes, len(row_arrays)),
        [((NP, NV), bf16), ((NV, NV), bf16), ((NV, HALF_V), f32)],
        [place, *row_arrays, own_cols, other_cols, row_energy, col_energy],
        [((NP, NV), bf16), ((NV, 1), f32), ((1, NV), f32)],
        dot * (NP + HALF_V),
        len(row_arrays) + 4,
        NO + 4,
        pltpu.HBM,
    )
    vir_got = swap(vir_give, "c")
    three_give, three_keep = call(
        give_and_keep,
        [((HALF_P, NV), f32)] * 2,
        [place, rows, amp],
        flops=dot * NP,
    )
    vir_got, three_give = lax.optimization_barrier((vir_got, three_give))
    three_got = swap(three_give, "c")
    (packed,) = call(
        pack_virtual,
        [((NO, VW + 8, HALF_V), f32)],
        [place, amp, vir_got],
        [((NV, HALF_V), f32)],
        dot * HALF_V,
    )
    packed, three_keep = lax.optimization_barrier((packed.astype(jnp.float16), three_keep))
    met = lax.all_to_all(packed, OCC, split_axis=0, concat_axis=0, tiled=True)
    own_piece, pieces = call(
        add_three,
        [((PW, NV), f32), ((Y * XH - 1, PW + 8, NV), f32)],
        [place, three_keep, three_got],
        [((HALF_P, NV), f32)] * 2,
        anywhere=2,
        n_sems=2,
    )
    got = [next_chip(piece.astype(jnp.float16), hop) for hop, piece in enumerate(pieces, 1)]
    met, *got[3:] = lax.optimization_barrier((met, *got[3:]))
    vir = jnp.sum(met[:, :VW].astype(f32) * weight_of(met, VW), 0)
    vir, *got[3:] = lax.optimization_barrier((vir, *got[3:]))
    got = [piece.astype(f32) for piece in got]
    (three,) = call(sum_three, [((PW, NV), f32)], [own_piece, *got])
    three_index = three[:, None, :]

    vir = vir.reshape(NO, VW // NO, HALF_V)
    vir = lax.all_to_all(vir, AUX, split_axis=0, concat_axis=0, tiled=True)
    vir = jnp.sum(vir.reshape(Y * XH, C, VW // NO, HALF_V), 0)
    vir_rows = jnp.concatenate([vir[0], vir[1]], 1)
    return (three_index, vir_rows / (NO * NV))


def solution(mesh):
    fine = Mesh(mesh.devices.reshape(XL, Z, Y, XH, C), ALL)
    return jax.shard_map(
        per_device,
        mesh=fine,
        in_specs=(P(None, AUX, None), P(None, OCC), P(), P()),
        out_specs=(P(AUX, OCC, None), P(ALL, None)),
        check_vma=False,
    )
```

```python
import functools

import jax
import jax.numpy as jnp
import numpy as np
from jax import lax
from jax.experimental import pallas as pl
from jax.experimental.pallas import tpu as pltpu
from jax.sharding import Mesh, PartitionSpec as P

OCC = ("xl", "z")
CHIPS = ("y", "xh")
AUX = ("y", "xh", "c")
ALL = OCC + AUX
XL, Z, Y, XH, C = 2, 8, 4, 2, 2
NO, NV, NP = 16, 768, 1024
PW, VW = 64, 48
VMEM = pl.BlockSpec(memory_space=pltpu.VMEM)
SMEM = pl.BlockSpec(memory_space=pltpu.SMEM)


def swap(array, axis):
    return lax.ppermute(array, axis, [(0, 1), (1, 0)])


def ring(array, by):
    pairs = [
        (z * C + c, (z + (1 - 2 * c) * by) % Z * C + c) for z in range(Z) for c in range(C)
    ]
    return lax.ppermute(array, ("z", "c"), pairs)


def next_chip(array, hop):
    pairs = [(q * C + c, hop_from(q, hop, c) * C + c) for q in range(Y * XH) for c in range(C)]
    return lax.ppermute(array, AUX, pairs)


def hop_from(q, hop, c):
    return (q // XH + (1 - 2 * c) * (hop // XH)) % Y * XH + (q + hop) % XH


def paced(array, us):
    def kernel(given, out):
        out[...] = given[...]

    return pl.pallas_call(
        kernel,
        out_shape=jax.ShapeDtypeStruct(array.shape, array.dtype),
        in_specs=[VMEM],
        out_specs=VMEM,
        compiler_params=pltpu.CompilerParams(vmem_limit_bytes=2**20),
        cost_estimate=pl.CostEstimate(flops=us * 10**9, bytes_accessed=2**20, transcendentals=0),
    )(array)


TRANSPOSED = (((0,), (0,)), ((), ()))
HALF_P, HALF_V = NP // C, NV // C


def amplitudes(n_rows, place, *refs):
    row_refs, (own_cols, other_cols, row_energy, col_energy) = refs[:n_rows], refs[n_rows : n_rows + 4]
    rows, amp, vir, cols, row_side, col_side, sems = refs[n_rows + 4 :]
    core = place[24]
    moves = []
    for ref in row_refs:
        for part in range(ref.shape[0] // PW):
            start = pl.multiple_of(place[len(moves)], PW)
            moves.append((ref.at[pl.ds(part * PW, PW)], rows.at[pl.ds(start, PW)]))
    for ref, side in ((own_cols, core), (other_cols, 1 - core)):
        moves.append((ref, cols.at[pl.ds(pl.multiple_of(side * HALF_P, HALF_P), HALF_P)]))
    moves += [(row_energy, row_side), (col_energy, col_side)]
    copies = [pltpu.make_async_copy(f, t, sems.at[k]) for k, (f, t) in enumerate(moves)]
    for copy in copies:
        copy.start()
    for copy in copies:
        copy.wait()
    for k in range(NV // 384):
        here = slice(k * 384, (k + 1) * 384)
        coulomb = lax.dot_general(
            rows[:, here], cols[...], TRANSPOSED, preferred_element_type=jnp.float32
        )
        amp[here, :] = (coulomb / (row_side[here, :] - col_side[...])).astype(jnp.bfloat16)
    virtual_block(amp, 1 - core, vir)


def virtual_block(amp, half, vir):
    side = amp[:, pl.ds(pl.multiple_of(half * HALF_V, HALF_V), HALF_V)]
    for k in range(NV // 384):
        here = slice(k * 384, (k + 1) * 384)
        vir[here, :] = lax.dot_general(
            amp[:, here], side, TRANSPOSED, preferred_element_type=jnp.float32
        )


def give_and_keep(place, rows, amp, give, keep):
    core = place[24]
    for out, side in ((give, 1 - core), (keep, core)):
        start = pl.multiple_of(side * HALF_P, HALF_P)
        out[...] = jnp.dot(rows[pl.ds(start, HALF_P), :], amp[...], preferred_element_type=jnp.float32)


def pack_virtual(place, amp, got, out, total):
    virtual_block(amp, place[24], total)
    total[...] += got[...]
    scale, power = scale_of(total[...])
    tail = jnp.broadcast_to(power, (8, HALF_V))
    for g in range(NO):
        out[g, :VW, :] = total[VW * g : VW * g + VW, :] * scale
        out[g, VW:, :] = tail


def add_three(place, keep, got, own, out, kept, met, sems):
    copies = [pltpu.make_async_copy(keep, kept, sems.at[0]), pltpu.make_async_copy(got, met, sems.at[1])]
    for copy in copies:
        copy.start()
    for copy in copies:
        copy.wait()
    kept[...] += met[...]
    scale, power = scale_of(kept[...])
    own[...] = kept[pl.ds(pl.multiple_of(place[16], PW), PW), :]
    for hop in range(1, Y * XH):
        out[hop - 1, :PW, :] = kept[pl.ds(pl.multiple_of(place[16 + hop], PW), PW), :] * scale
        out[hop - 1, PW:, :] = jnp.broadcast_to(power, (8, NV))


def sum_three(own, *refs):
    *got, out = refs
    total = own[...]
    for ref in got:
        total += ref[:PW, :] * jnp.exp2(ref[PW : PW + 1, :] - SCALE)
    out[...] = total


def scale_of(total):
    top = jnp.maximum(jnp.max(jnp.abs(total), keepdims=True), 2.0**-100)
    power = jnp.ceil(jnp.log2(top))
    return jnp.exp2(SCALE - power), power


def weight_of(sent, rows):
    power = lax.optimization_barrier(sent[..., rows : rows + 1, :])
    return jnp.exp2(power.astype(jnp.float32) - SCALE)


SCALE = 14.0
PACE = 25


def call(kernel, shapes, args, scratch=(), flops=0, anywhere=0, n_sems=0, space=pl.ANY):
    spaces = [SMEM if a.dtype == jnp.int32 else VMEM for a in args]
    first = 1 if args[0].dtype == jnp.int32 else 0
    spaces[first : first + anywhere] = [pl.BlockSpec(memory_space=space)] * anywhere
    sems = [pltpu.SemaphoreType.DMA((n_sems,))] if n_sems else []
    return pl.pallas_call(
        kernel,
        out_shape=[jax.ShapeDtypeStruct(s, t) for s, t in shapes],
        in_specs=spaces,
        out_specs=[VMEM] * len(shapes),
        scratch_shapes=[pltpu.VMEM(s, t) for s, t in scratch] + sems,
        compiler_params=pltpu.CompilerParams(vmem_limit_bytes=16 * 2**20),
        cost_estimate=pl.CostEstimate(flops=flops, bytes_accessed=6 * 2**20, transcendentals=0),
    )(*args)


def per_device(half_integrals, vir_coef, occ_energy, vir_energy):
    xl, z, y, xh, c = (lax.axis_index(n) for n in ALL)
    own = xl * Z + z
    chip = y * XH + xh
    native = jnp.einsum(
        "ipm,ma->ipa", half_integrals, vir_coef, preferred_element_type=jnp.float32
    ).astype(jnp.bfloat16)

    flat = jnp.transpose(native, (1, 0, 2)).reshape(PW, NV)
    pair = jnp.concatenate(
        [
            lax.ppermute(flat, ALL, [(o * NO + x, (x ^ flip) * NO + o) for o in range(NO) for x in range(NO)])
            for flip in (0, Z)
        ],
        0,
    )
    slice_energy = lax.dynamic_slice_in_dim(vir_energy, (chip * C + c) * VW, VW, 0)
    own_energy = lax.dynamic_slice_in_dim(occ_energy, own, 1, 0)
    row_energy = ((own_energy + occ_energy)[:, None] - slice_energy[None, :]).reshape(NV, 1)
    col_energy = vir_energy[None, :]

    local = lax.all_to_all(native, OCC, split_axis=0, concat_axis=0, tiled=True)
    row_energy = paced(row_energy, PACE)
    pair, local, row_energy = lax.optimization_barrier((pair, local, row_energy))
    local = jnp.transpose(local, (1, 0, 2)).reshape(PW, NV)
    up1, down1, up2, down2 = (ring(pair, by) for by in (1, -1, 2, -2))
    own_cols = lax.all_to_all(
        jnp.broadcast_to(local, (Y * XH, PW, NV)), CHIPS, split_axis=0, concat_axis=0, tiled=True
    ).reshape(HALF_P, NV)
    row_energy, col_energy, local = lax.optimization_barrier((row_energy, col_energy, local))
    col_energy = paced(col_energy, PACE)
    up2, down2, col_energy = lax.optimization_barrier((up2, down2, col_energy))
    col_energy = paced(col_energy, PACE)
    up3, down3, far = ring(up2, 1), ring(down2, -1), ring(up2, 2)
    other_cols = swap(own_cols, "c")
    row_arrays = [pair, up1, down1, up2, down2, up3, down3, far]
    owners = []
    for step in (0, -1, 1, -2, 2, -3, 3, Z // 2):
        at = (z + (1 - 2 * c) * step) % Z
        owners += [xl * Z + at, (1 - xl) * Z + at]
    places = [o % C * HALF_P + o // C * PW for o in owners]
    places += [hop_from(chip, hop, c) * PW for hop in range(Y * XH)] + [c]
    place = jnp.stack(places).astype(jnp.int32)

    bf16, f32 = jnp.bfloat16, jnp.float32
    dot = 2 * NV * NV
    rows, amp, vir_give = call(
        functools.partial(amplitudes, len(row_arrays)),
        [((NP, NV), bf16), ((NV, NV), bf16), ((NV, HALF_V), f32)],
        [place, *row_arrays, own_cols, other_cols, row_energy, col_energy],
        [((NP, NV), bf16), ((NV, 1), f32), ((1, NV), f32)],
        dot * (NP + HALF_V),
        len(row_arrays) + 4,
        NO + 4,
        pltpu.HBM,
    )
    vir_got = swap(vir_give, "c")
    three_give, three_keep = call(
        give_and_keep,
        [((HALF_P, NV), f32)] * 2,
        [place, rows, amp],
        flops=dot * NP,
    )
    vir_got, three_give = lax.optimization_barrier((vir_got, three_give))
    three_got = swap(three_give, "c")
    (packed,) = call(
        pack_virtual,
        [((NO, VW + 8, HALF_V), f32)],
        [place, amp, vir_got],
        [((NV, HALF_V), f32)],
        dot * HALF_V,
    )
    packed, three_keep = lax.optimization_barrier((packed.astype(jnp.float16), three_keep))
    met = lax.all_to_all(packed, OCC, split_axis=0, concat_axis=0, tiled=True)
    own_piece, pieces = call(
        add_three,
        [((PW, NV), f32), ((Y * XH - 1, PW + 8, NV), f32)],
        [place, three_keep, three_got],
        [((HALF_P, NV), f32)] * 2,
        anywhere=2,
        n_sems=2,
    )
    got = [next_chip(piece.astype(jnp.float16), hop) for hop, piece in enumerate(pieces, 1)]
    met, *got[4:] = lax.optimization_barrier((met, *got[4:]))
    vir = jnp.sum(met[:, :VW].astype(f32) * weight_of(met, VW), 0)
    vir, *got[4:] = lax.optimization_barrier((vir, *got[4:]))
    got = [piece.astype(f32) for piece in got]
    (three,) = call(sum_three, [((PW, NV), f32)], [own_piece, *got])
    three_index = three[:, None, :]

    vir = vir.reshape(NO, VW // NO, HALF_V)
    vir = lax.all_to_all(vir, AUX, split_axis=0, concat_axis=0, tiled=True)
    vir = jnp.sum(vir.reshape(Y * XH, C, VW // NO, HALF_V), 0)
    vir_rows = jnp.concatenate([vir[0], vir[1]], 1)
    return (three_index, vir_rows / (NO * NV))


def solution(mesh):
    fine = Mesh(mesh.devices.reshape(XL, Z, Y, XH, C), ALL)
    return jax.shard_map(
        per_device,
        mesh=fine,
        in_specs=(P(None, AUX, None), P(None, OCC), P(), P()),
        out_specs=(P(AUX, OCC, None), P(ALL, None)),
        check_vma=False,
    )
```
